32 devices in a mesh: parts: 2 (over y), dp: 4 (over z), mp: 4 (over x, core).
Axes of the slice: x: 2, y: 2, z: 4, core: 2. Of those that a mesh axis runs over, the one named last changes fastest.
Arguments:
- tokens: bfloat16 [8192, 8192], P(('parts', 'dp'), 'mp'), parts along dimension 0, may hold values from -6 to 6
- input_norm_weight: bfloat16 [8192], P('mp'), may hold values from 0.25 to 1.75
- value_weight: bfloat16 [8192, 1024], P('mp'), may hold values from -0.09375 to 0.09375
- adapter_down_weight: bfloat16 [4, 8192, 64], P('dp', 'mp'), may hold values from -0.0625 to 0.0625
- adapter_up_weight: bfloat16 [4, 64, 1024], P('dp', None, 'mp'), may hold values from -0.75 to 0.75
- tile_owner_adapter: int32 [64], P(('parts', 'dp')), parts along dimension 0, may hold values from 0 to 3
- request_tile_count: int32 [8], P(('parts', 'dp')), parts along dimension 0, may hold values from 1 to 8
- adapter_storage_slot: int32 [4], replicated, may hold values from 0 to 3, each once
Outputs:
- values: bfloat16 [8192, 1024], P(('parts', 'dp'), 'mp'), parts along dimension 0
The draws below stay inside these ranges and needn't reach their ends.
There are 2 independent parts, one for each index of `parts`. The reference program is written for one: setup_inputs(seed, part) draws one part's arguments, and reference() takes and returns one part's arrays. A program takes and returns all parts, laid end to end along the dimension named above; an argument that names none is the same for every part. Nothing has to cross between parts.
Inputs may be any that keep to these rules, and one draw needn't show every extreme that they name: Adapter a is stored at index adapter_storage_slot[a] of adapter_down_weight and adapter_up_weight; each slot holds one adapter.
All inputs are finite; a program needn't handle non-finite values.
Results may differ from the reference program's by a relative error of at most 0.012.
Values may be sent and summed in bfloat16 or wider, within the bound.
A program may use at most 64 MiB of HBM per device.

```python
import math
import jax
import jax.numpy as jnp
import numpy as np
from jax import lax

MODEL_WIDTH = 8192
VALUE_WIDTH = 1024
ADAPTER_RANK = 64
REWARD_ADAPTERS = 4
TILES = 8
TOKENS = 4096
NTILES = 32
N_DP = 4
N_MP = 4


def plant(values, rng, low, largest):
    shape = values.shape
    index_at = [jax.random.randint(jax.random.fold_in(rng, axis), (), 0, shape[axis]) for axis in range(len(shape))]
    values = values.at[tuple(index_at)].set(low)
    longest = shape.index(max(shape))
    index_at[longest] = (index_at[longest] + 1) % shape[longest]
    return values.at[tuple(index_at)].set(largest)


def with_spikes(drawn, key, source, target, blocks, factor):
    def block_of(position):
        return (jnp.arange(drawn.shape[position]) // (drawn.shape[position] // blocks)).reshape((-1,) + (1,) * (drawn.ndim - 1 - position))

    one_side = jax.random.permutation(key, blocks)[block_of(target)]
    second = (block_of(target) + blocks // 2) % blocks
    return jnp.where((block_of(source) == one_side) | (block_of(source) == second), factor * drawn, drawn)


def steps_of(key, dims, split, least, high):
    loudness = 1.0
    for axis_at, parts in split:
        draws = jax.random.uniform(jax.random.fold_in(jax.random.fold_in(key, 6), axis_at), (parts,), jnp.float32, least / len(split), high / len(split))
        loudness = loudness * jnp.repeat(jnp.exp(draws), dims[axis_at] // parts).reshape((-1,) + (1,) * (len(dims) - 1 - axis_at))
    return loudness


def cumulative_ranks(count, slope):
    portions = [(1 << 20) // math.isqrt(grade ** slope) + 1 for grade in range(1, count + 1)]
    spread = 1 + sum(portions) // (1 << 30)
    return np.cumsum(np.array([max(1, weight // spread) for weight in portions]))


def skewed_ids(own_key, extent, amount, lean):
    table = cumulative_ranks(amount, lean)
    ticket = jax.random.randint(jax.random.fold_in(own_key, 1), extent, 0, int(table[amount - 1]))
    grade = jnp.searchsorted(jnp.asarray(table, jnp.int32), ticket, side="right")
    return jax.random.permutation(jax.random.fold_in(own_key, 2), amount)[grade].astype(jnp.int32)


def normal_values(own_key, dims, deviation, most, split=(), held_as=jnp.bfloat16):
    result = jax.random.normal(own_key, dims, jnp.float32) * deviation
    if len(split) > 0:
        result = steps_of(own_key, dims, split, -0.22, 0.18) * result
    return jnp.clip(result, min=-most, max=most).astype(held_as)


def heavy_noise(stream_key, shape, deviation, bound, cuts, heavy, kind=jnp.bfloat16):
    entries = deviation * jax.random.normal(stream_key, shape, jnp.float32)
    if cuts:
        entries = entries * steps_of(stream_key, shape, cuts, -0.22, 0.18)
    return jnp.clip(with_spikes(entries, jax.random.fold_in(stream_key, 3), *heavy), -bound, bound).astype(kind)


def setup_inputs(seed: int = 0, part: int = 0) -> dict:
    seeds = jax.random.split(jax.random.key(seed), 9)
    own_keys = jax.random.split(jax.random.fold_in(seeds[8], part), 9)
    tokens = normal_values(own_keys[0], (TOKENS, MODEL_WIDTH), 1.0, 6.0, ((0, 4), (1, 4)))
    input_norm_weight = jnp.clip(1.0 + 0.15 * jax.random.normal(seeds[1], (MODEL_WIDTH,), jnp.float32), 0.25, 1.75).astype(jnp.bfloat16)
    value_weight = heavy_noise(seeds[2], (MODEL_WIDTH, VALUE_WIDTH), MODEL_WIDTH ** -0.5, 0.09375, ((0, 4),), (0, 1, 4, 2.0))
    adapter_down_weight = normal_values(seeds[3], (REWARD_ADAPTERS, MODEL_WIDTH, ADAPTER_RANK), MODEL_WIDTH ** -0.5, 0.0625, ((0, 4), (1, 4)))
    adapter_up_weight = normal_values(seeds[4], (REWARD_ADAPTERS, ADAPTER_RANK, VALUE_WIDTH), ADAPTER_RANK ** -0.5, 0.75, ((0, 4), (2, 4)))
    tile_owner_adapter = plant(skewed_ids(own_keys[5], (NTILES,), REWARD_ADAPTERS, 2), jax.random.fold_in(own_keys[5], 3), 0, REWARD_ADAPTERS - 1).astype(jnp.int32)
    request_tile_count = plant(jax.random.randint(own_keys[6], (N_DP,), 1, TILES + 1), jax.random.fold_in(own_keys[6], 1), 1, TILES).astype(jnp.int32)
    adapter_storage_slot = jax.random.permutation(seeds[7], REWARD_ADAPTERS).astype(jnp.int32)
    return dict(tokens=tokens, input_norm_weight=input_norm_weight, value_weight=value_weight, adapter_down_weight=adapter_down_weight, adapter_up_weight=adapter_up_weight, tile_owner_adapter=tile_owner_adapter, request_tile_count=request_tile_count, adapter_storage_slot=adapter_storage_slot)


def reference(tokens, input_norm_weight, value_weight, adapter_down_weight, adapter_up_weight, tile_owner_adapter, request_tile_count, adapter_storage_slot):
    floats = tokens.astype(jnp.float32)
    inv_rms = lax.rsqrt(lax.optimization_barrier(jnp.mean(floats * floats, axis=1)) + 1e-05)
    normed = (floats * inv_rms[:, None] * input_norm_weight.astype(jnp.float32)[None, :]).astype(jnp.bfloat16)
    block = MODEL_WIDTH // N_MP
    base = jnp.zeros((TOKENS, VALUE_WIDTH), jnp.float32)
    for index in range(N_MP):
        partial_sum = jnp.dot(normed[:, index * block:(index + 1) * block], value_weight[index * block:(index + 1) * block, :], preferred_element_type=jnp.float32)
        base = base + partial_sum.astype(jnp.bfloat16).astype(jnp.float32)
    slot = adapter_storage_slot[tile_owner_adapter].astype(jnp.int32)
    tile_grouped = normed.reshape(NTILES, 128, MODEL_WIDTH)

    def one_tile(packed):
        rows, selected_adapter = packed
        down_matrix = lax.dynamic_index_in_dim(adapter_down_weight, selected_adapter, 0, keepdims=False)
        up_matrix = lax.dynamic_index_in_dim(adapter_up_weight, selected_adapter, 0, keepdims=False).astype(jnp.float32)
        low = jnp.dot(rows, down_matrix, preferred_element_type=jnp.float32)
        return 2.0 * jnp.dot(low, up_matrix, precision=lax.Precision.HIGHEST)
    delta = lax.map(one_tile, (tile_grouped, slot)).reshape(TOKENS, VALUE_WIDTH)
    tile_index = jnp.arange(NTILES, dtype=jnp.int32)
    alive = tile_index % TILES < request_tile_count[tile_index // TILES]
    alive_rows = jnp.repeat(alive, 128)
    return jnp.where(alive_rows[:, None], base + delta, 0.0).astype(jnp.bfloat16)
```

```python
import functools

import jax
import jax.numpy as jnp
from jax import lax
from jax.experimental import pallas as pl
from jax.experimental.pallas import tpu as pltpu
from jax.sharding import PartitionSpec as P

TILE = 128
CORES = 2
MESH = pl.DeviceIdType.MESH
F32 = jnp.float32
BF16 = jnp.bfloat16


def kernel(
    sizes,
    owner_ref,
    count_ref,
    store_ref,
    tok_hbm,
    gain_ref,
    w_hbm,
    down_ref,
    up_ref,
    out_ref,
    tok,
    scaled,
    w,
    gath,
    pair_out,
    pair_in,
    acc,
    far_out,
    far_in,
    sq_cols,
    sq,
    low_sel,
    low_pack,
    low_pair,
    low_far_out,
    low_far_in,
    low_done,
    tok_sem,
    w_sem,
    pair_s,
    pair_r,
    far_s,
    far_r,
    sq_s,
    sq_r,
    up_s,
    dn_s,
    z_r,
    part_s,
    part_r,
    low_s,
    low_r,
    lowx_s,
    lowx_r,
):
    n_parts, n_dp, n_mp, chunk = sizes
    rows, feats = tok.shape
    block = w.shape[2]
    rank = down_ref.shape[1]
    lanes = 2 * rank
    xs = n_mp // CORES
    chunks = rows // chunk
    tiles = rows // TILE
    me_p, me_z, me = lax.axis_index("parts"), lax.axis_index("dp"), lax.axis_index("mp")
    x, c = me // CORES, me % CORES
    mate = x * CORES + (1 - c)

    def far_id(d):
        return lax.rem(x + d, xs) * CORES + c

    def col(d, core):
        return lax.rem(x + d, xs) * CORES + core

    def tok_copy(i):
        at = pl.ds(pl.multiple_of(i * chunk, chunk), chunk)
        return pltpu.make_async_copy(tok_hbm.at[at], tok.at[at], tok_sem.at[i])

    def w_copy(k, index):
        at = pl.ds(pl.multiple_of(index * block, block), block)
        return pltpu.make_async_copy(w_hbm.at[:, at], w.at[k], w_sem.at[k])

    order = list(range(1, xs)) + [0]
    w_list = []
    for d in order:
        for core in (1 - c, c):
            w_list.append((len(w_list), col(d, core)))
    tok_copy(0).start()
    w_copy(*w_list[0]).start()
    w_copy(*w_list[1]).start()
    for i in range(1, chunks):
        tok_copy(i).start()
    for item in w_list[2:]:
        w_copy(*item).start()

    barrier = pltpu.get_barrier_semaphore()
    has_up = me_z < n_dp - 1
    has_dn = me_z > 0
    for k in range(1, n_mp):
        pl.semaphore_signal(
            barrier, inc=1, device_id={"mp": lax.rem(me + k, n_mp)}, device_id_type=MESH
        )
    for k in range(1, n_parts):
        pl.semaphore_signal(
            barrier, inc=1, device_id={"parts": lax.rem(me_p + k, n_parts)}, device_id_type=MESH
        )

    @pl.when(has_up)
    def _():
        pl.semaphore_signal(barrier, inc=1, device_id={"dp": me_z + 1}, device_id_type=MESH)

    @pl.when(has_dn)
    def _():
        pl.semaphore_signal(barrier, inc=1, device_id={"dp": me_z - 1}, device_id_type=MESH)

    chain = has_up.astype(jnp.int32) + has_dn.astype(jnp.int32)
    pl.semaphore_wait(barrier, n_mp - 1 + n_parts - 1 + chain)

    own_rows = pl.ds(pl.multiple_of(me_z * rank, rank), rank)
    gath[own_rows, :feats] = down_ref[0]
    gath[own_rows, feats:] = up_ref[0]
    piece = rank // n_parts

    def part_of(a, p):
        return gath.at[pl.ds(pl.multiple_of(a * rank + p * piece, 16), piece)]

    def z_copy(a, to, sems):
        ref = part_of(a, me_p)
        return pltpu.make_async_remote_copy(
            ref, ref, sems.at[a], z_r.at[a], device_id={"dp": to}, device_id_type=MESH
        )

    def part_copy(a, k):
        ref = part_of(a, me_p)
        return pltpu.make_async_remote_copy(
            ref,
            ref,
            part_s.at[a, k],
            part_r.at[a, k],
            device_id={"parts": lax.rem(me_p + k, n_parts)},
            device_id_type=MESH,
        )

    @pl.when(has_up)
    def _():
        z_copy(me_z, me_z + 1, up_s).start()

    @pl.when(has_dn)
    def _():
        z_copy(me_z, me_z - 1, dn_s).start()

    def relay(k):
        below, above = me_z - k, me_z + k

        @pl.when(below >= 0)
        def _():
            z_copy(below, me_z, up_s).wait_recv()

            @pl.when(has_up)
            def _():
                z_copy(below, me_z + 1, up_s).start()

            for q in range(1, n_parts):
                part_copy(below, q).start()

        @pl.when(above < n_dp)
        def _():
            z_copy(above, me_z, dn_s).wait_recv()

            @pl.when(has_dn)
            def _():
                z_copy(above, me_z - 1, dn_s).start()

            for q in range(1, n_parts):
                part_copy(above, q).start()

    def pair_copy(d, i):
        at = pl.ds(pl.multiple_of(i * chunk, chunk), chunk)
        return pltpu.make_async_remote_copy(
            pair_out.at[d, at],
            pair_in.at[d, at],
            pair_s.at[d, i],
            pair_r.at[d, i],
            device_id={"mp": mate},
            device_id_type=MESH,
        )

    def far_copy(d, i):
        at = pl.ds(pl.multiple_of(i * chunk, chunk), chunk)
        return pltpu.make_async_remote_copy(
            far_out.at[d - 1, at],
            far_in.at[d - 1, at],
            far_s.at[d - 1, i],
            far_r.at[d - 1, i],
            device_id={"mp": far_id(d)},
            device_id_type=MESH,
        )

    def forward(d, i):
        at = pl.ds(pl.multiple_of(i * chunk, chunk), chunk)
        pair_copy(d, i).wait_recv()
        far_out[d - 1, at] = (acc[d, at] + pair_in[d, at].astype(F32)).astype(BF16)
        far_copy(d, i).start()

    for n, d in enumerate(order):
        for k in (0, 1):
            w_copy(*w_list[2 * n + k]).wait()

        def step(i, carry, n=n, d=d):
            at = pl.ds(pl.multiple_of(i * chunk, chunk), chunk)
            if n == 0:
                tok_copy(i).wait()
                scaled[at] = tok[at] * gain_ref[...]
            pair_out[d, at] = jnp.dot(
                scaled[at], w[2 * n], preferred_element_type=F32
            ).astype(BF16)
            pair_copy(d, i).start()
            acc[d, at] = jnp.dot(scaled[at], w[2 * n + 1], preferred_element_type=F32)
            if d > 0:

                @pl.when(i > 0)
                def _():
                    forward(d, i - 1)

            return carry

        lax.fori_loop(0, chunks, step, 0)
        if d > 0:
            forward(d, chunks - 1)
        if n == 0:
            relay(1)

            def squares(i, carry):
                at = pl.ds(pl.multiple_of(i * 32, 32), 32)
                t = tok[at].astype(F32)
                sq_cols[at] = jnp.broadcast_to(
                    jnp.sum(t * t, axis=1, keepdims=True), (32, TILE)
                )
                return carry

            lax.fori_loop(0, rows // 32, squares, 0)
            for t in range(tiles):
                sq[0, t : t + 1, :] = sq_cols[t * TILE : (t + 1) * TILE, :].T[0:1, :]
            for k in range(1, n_mp):
                sq_copy(sq, sq_s, sq_r, me, n_mp, k).start()
    for k in range(2, n_dp):
        relay(k)

    for a in range(n_dp):

        @pl.when(me_z != a)
        def _(a=a):
            for q in range(1, n_parts):
                other = lax.rem(me_p + n_parts - q, n_parts)
                ref = part_of(a, other)
                pltpu.make_async_remote_copy(
                    ref,
                    ref,
                    part_s.at[a, q],
                    part_r.at[a, q],
                    device_id={"parts": lax.rem(me_p + q, n_parts)},
                    device_id_type=MESH,
                ).wait_recv()

    lane = lax.broadcasted_iota(jnp.int32, (TILE, lanes), 1)
    upper = lane >= rank
    slots = [store_ref[owner_ref[t]] for t in range(tiles)]

    def low_step(t, carry):
        at = pl.ds(pl.multiple_of(t * TILE, TILE), TILE)
        slot = store_ref[owner_ref[t]]
        low = lax.dot_general(
            scaled[at], gath[:, :feats], (((1,), (1,)), ((), ())), preferred_element_type=F32
        )
        picked = jnp.zeros((TILE, lanes), F32)
        for g in range(n_dp // 2):
            picked = jnp.where(
                2 * g + upper.astype(jnp.int32) == slot,
                low[:, g * lanes : (g + 1) * lanes],
                picked,
            )
        low_sel[at] = picked + pltpu.roll(picked, rank, 1)
        return carry

    lax.fori_loop(0, tiles, low_step, 0)
    quarter = tiles // 4
    for h in range(CORES):
        for q in range(quarter):
            first = h * (tiles // 2) + q
            second = first + quarter
            low_pack[h, q * TILE : (q + 1) * TILE, :] = jnp.where(
                upper,
                low_sel[second * TILE : (second + 1) * TILE, :],
                low_sel[first * TILE : (first + 1) * TILE, :],
            ).astype(BF16)
    to_mate = pltpu.make_async_remote_copy(
        low_pack.at[1 - c],
        low_pair,
        low_s.at[0],
        low_r.at[0],
        device_id={"mp": mate},
        device_id_type=MESH,
    )
    to_mate.start()
    to_mate.wait_recv()
    low_far_out[...] = (low_pack[c].astype(F32) + low_pair[...].astype(F32)).astype(BF16)

    def low_far(d):
        return pltpu.make_async_remote_copy(
            low_far_out,
            low_far_in.at[d - 1],
            lowx_s.at[d - 1],
            lowx_r.at[d - 1],
            device_id={"mp": far_id(d)},
            device_id_type=MESH,
        )

    for d in range(1, xs):
        low_far(d).start()

    for i in range(chunks):
        at = pl.ds(i * chunk, chunk)
        pair_copy(0, i).wait_recv()
        acc[0, at] = acc[0, at] + pair_in[0, at].astype(F32)
    total = sq[0]
    for k in range(1, n_mp):
        sq_copy(sq, sq_s, sq_r, me, n_mp, k).wait_recv()
        total = total + sq[k]
    inv = lax.rsqrt(total / (feats * n_mp) + 1e-05)
    sq_cols[...] = jnp.concatenate(
        [jnp.broadcast_to(inv[t : t + 1, :], (TILE, TILE)).T for t in range(tiles)], axis=0
    )

    low_sum = low_far_out[...].astype(F32)
    for d in range(1, xs):
        low_far(d).wait_recv()
        low_sum = low_sum + low_far_in[d - 1].astype(F32)
    low_done[c] = low_sum.astype(BF16)
    done = pltpu.make_async_remote_copy(
        low_done.at[c],
        low_done.at[c],
        low_s.at[1],
        low_r.at[1],
        device_id={"mp": mate},
        device_id_type=MESH,
    )
    done.start()
    pltpu.make_async_remote_copy(
        low_done.at[1 - c],
        low_done.at[1 - c],
        low_s.at[1],
        low_r.at[1],
        device_id={"mp": mate},
        device_id_type=MESH,
    ).wait_recv()

    for t in range(tiles):
        at = slice(t * TILE, (t + 1) * TILE)
        h, j = t // (tiles // 2), t % (tiles // 2)
        q, second = j % quarter, j >= quarter
        packed = low_done[h, q * TILE : (q + 1) * TILE, :].astype(F32)
        rolled = pltpu.roll(packed, rank, 1)
        own = jnp.where(upper, packed, rolled) if second else jnp.where(upper, rolled, packed)
        spread = jnp.concatenate(
            [
                jnp.where(2 * g + upper.astype(jnp.int32) == slots[t], own, 0.0)
                for g in range(n_dp // 2)
            ],
            axis=1,
        ).astype(BF16)
        delta = jnp.dot(spread, gath[:, feats:], preferred_element_type=F32)
        acc[0, at] = acc[0, at] + 2.0 * delta

    for i in range(chunks):
        for d in range(1, xs):
            far_copy(d, i).wait_recv()
        for t in range(i * chunk // TILE, (i + 1) * chunk // TILE):
            at = slice(t * TILE, (t + 1) * TILE)
            value = acc[0, at]
            for d in range(1, xs):
                value = value + far_in[d - 1, at].astype(F32)
            scale = jnp.concatenate([sq_cols[at, :]] * (block // TILE), axis=1)
            out_ref[at, :] = jnp.where(t < count_ref[0], value * scale, 0.0).astype(BF16)

    for d in order:
        for i in range(chunks):
            pair_copy(d, i).wait_send()
            if d > 0:
                far_copy(d, i).wait_send()
    for k in range(1, n_mp):
        sq_copy(sq, sq_s, sq_r, me, n_mp, k).wait_send()
    to_mate.wait_send()
    done.wait_send()
    for d in range(1, xs):
        low_far(d).wait_send()
    for a in range(n_dp):

        @pl.when(jnp.logical_and(has_up, a <= me_z))
        def _(a=a):
            z_copy(a, me_z, up_s).wait_send()

        @pl.when(jnp.logical_and(has_dn, a >= me_z))
        def _(a=a):
            z_copy(a, me_z, dn_s).wait_send()

        @pl.when(me_z != a)
        def _(a=a):
            for q in range(1, n_parts):
                part_copy(a, q).wait_send()


def sq_copy(sq, sq_s, sq_r, me, n_mp, k):
    return pltpu.make_async_remote_copy(
        sq.at[0],
        sq.at[k],
        sq_s.at[k],
        sq_r.at[k],
        device_id={"mp": lax.rem(me + k, n_mp)},
        device_id_type=MESH,
    )


def shards(mesh, tokens, gain, weight, down, up, owner, count, store):
    n_parts, n_dp, n_mp = (mesh.shape[name] for name in ("parts", "dp", "mp"))
    rows, feats = tokens.shape
    cols = weight.shape[1]
    rank = down.shape[2]
    block = cols // n_mp
    xs = n_mp // CORES
    chunk = 256
    chunks = rows // chunk
    far = max(xs - 1, 1)
    low_rows = rows // 4
    vmem = pltpu.VMEM
    dma = pltpu.SemaphoreType.DMA
    smem = pl.BlockSpec(memory_space=pltpu.SMEM)
    in_vmem = pl.BlockSpec(memory_space=pltpu.VMEM)
    in_hbm = pl.BlockSpec(memory_space=pl.ANY)
    return pl.pallas_call(
        functools.partial(kernel, (n_parts, n_dp, n_mp, chunk)),
        out_shape=jax.ShapeDtypeStruct((rows, block), BF16),
        in_specs=[smem, smem, smem, in_hbm, in_vmem, in_hbm, in_vmem, in_vmem],
        out_specs=in_vmem,
        scratch_shapes=[
            vmem((rows, feats), BF16),
            vmem((rows, feats), BF16),
            vmem((n_mp, feats, block), BF16),
            vmem((n_dp * rank, feats + block), BF16),
            vmem((xs, rows, block), BF16),
            vmem((xs, rows, block), BF16),
            vmem((xs, rows, block), F32),
            vmem((far, rows, block), BF16),
            vmem((far, rows, block), BF16),
            vmem((rows, TILE), F32),
            vmem((n_mp, rows // TILE, TILE), F32),
            vmem((rows, 2 * rank), F32),
            vmem((CORES, low_rows, 2 * rank), BF16),
            vmem((low_rows, 2 * rank), BF16),
            vmem((low_rows, 2 * rank), BF16),
            vmem((far, low_rows, 2 * rank), BF16),
            vmem((CORES, low_rows, 2 * rank), BF16),
            dma((chunks,)),
            dma((n_mp,)),
            dma((xs, chunks)),
            dma((xs, chunks)),
            dma((far, chunks)),
            dma((far, chunks)),
            dma((n_mp,)),
            dma((n_mp,)),
            dma((n_dp,)),
            dma((n_dp,)),
            dma((n_dp,)),
            dma((n_dp, n_parts)),
            dma((n_dp, n_parts)),
            dma((2,)),
            dma((2,)),
            dma((far,)),
            dma((far,)),
        ],
        compiler_params=pltpu.CompilerParams(
            collective_id=0, has_side_effects=True, vmem_limit_bytes=56 * 1024 * 1024
        ),
    )(owner, count, store, tokens, gain.reshape(1, feats), weight, down.transpose(0, 2, 1), up)


def solution(mesh):
    in_specs = (
        P(("parts", "dp"), "mp"),
        P("mp"),
        P("mp", None),
        P("dp", "mp", None),
        P("dp", None, "mp"),
        P(("parts", "dp")),
        P(("parts", "dp")),
        P(),
    )
    out_specs = P(("parts", "dp"), "mp")
    return jax.shard_map(
        functools.partial(shards, mesh),
        mesh=mesh,
        in_specs=in_specs,
        out_specs=out_specs,
        check_vma=False,
    )
```

```python
import functools

import jax
import jax.numpy as jnp
from jax import lax
from jax.experimental import pallas as pl
from jax.experimental.pallas import tpu as pltpu
from jax.sharding import PartitionSpec as P

TILE = 128
CORES = 2
MESH = pl.DeviceIdType.MESH
F32 = jnp.float32
BF16 = jnp.bfloat16


def kernel(
    sizes,
    owner_ref,
    count_ref,
    store_ref,
    tok_hbm,
    gain_ref,
    w_hbm,
    down_ref,
    up_ref,
    out_ref,
    tok,
    scaled,
    w,
    gath,
    pair_out,
    pair_in,
    acc,
    far_out,
    far_in,
    sq_cols,
    sq,
    low_sel,
    low_pack,
    low_pair,
    low_far_out,
    low_far_in,
    low_done,
    tok_sem,
    w_sem,
    pair_s,
    pair_r,
    far_s,
    far_r,
    sq_s,
    sq_r,
    up_s,
    dn_s,
    z_r,
    part_s,
    part_r,
    low_s,
    low_r,
    lowx_s,
    lowx_r,
):
    n_parts, n_dp, n_mp, chunk = sizes
    rows, feats = tok.shape
    block = w.shape[2]
    rank = down_ref.shape[1]
    lanes = 2 * rank
    xs = n_mp // CORES
    chunks = rows // chunk
    tiles = rows // TILE
    me_p, me_z, me = lax.axis_index("parts"), lax.axis_index("dp"), lax.axis_index("mp")
    x, c = me // CORES, me % CORES
    mate = x * CORES + (1 - c)

    def far_id(d):
        return lax.rem(x + d, xs) * CORES + c

    def col(d, core):
        return lax.rem(x + d, xs) * CORES + core

    def tok_copy(i):
        at = pl.ds(pl.multiple_of(i * chunk, chunk), chunk)
        return pltpu.make_async_copy(tok_hbm.at[at], tok.at[at], tok_sem.at[i])

    def w_copy(k, index):
        at = pl.ds(pl.multiple_of(index * block, block), block)
        return pltpu.make_async_copy(w_hbm.at[:, at], w.at[k], w_sem.at[k])

    order = list(range(1, xs)) + [0]
    w_list = []
    for d in order:
        for core in (1 - c, c):
            w_list.append((len(w_list), col(d, core)))
    tok_copy(0).start()
    w_copy(*w_list[0]).start()
    w_copy(*w_list[1]).start()
    for i in range(1, chunks):
        tok_copy(i).start()
    for item in w_list[2:]:
        w_copy(*item).start()

    barrier = pltpu.get_barrier_semaphore()
    has_up = me_z < n_dp - 1
    has_dn = me_z > 0
    for k in range(1, n_mp):
        pl.semaphore_signal(
            barrier, inc=1, device_id={"mp": lax.rem(me + k, n_mp)}, device_id_type=MESH
        )
    for k in range(1, n_parts):
        pl.semaphore_signal(
            barrier, inc=1, device_id={"parts": lax.rem(me_p + k, n_parts)}, device_id_type=MESH
        )

    @pl.when(has_up)
    def _():
        pl.semaphore_signal(barrier, inc=1, device_id={"dp": me_z + 1}, device_id_type=MESH)

    @pl.when(has_dn)
    def _():
        pl.semaphore_signal(barrier, inc=1, device_id={"dp": me_z - 1}, device_id_type=MESH)

    chain = has_up.astype(jnp.int32) + has_dn.astype(jnp.int32)
    pl.semaphore_wait(barrier, n_mp - 1 + n_parts - 1 + chain)

    own_rows = pl.ds(pl.multiple_of(me_z * rank, rank), rank)
    gath[own_rows, :feats] = down_ref[0]
    gath[own_rows, feats:] = up_ref[0]
    piece = rank // n_parts

    def part_of(a, p):
        return gath.at[pl.ds(pl.multiple_of(a * rank + p * piece, 16), piece)]

    def z_copy(a, to, sems):
        ref = part_of(a, me_p)
        return pltpu.make_async_remote_copy(
            ref, ref, sems.at[a], z_r.at[a], device_id={"dp": to}, device_id_type=MESH
        )

    def part_copy(a, k):
        ref = part_of(a, me_p)
        return pltpu.make_async_remote_copy(
            ref,
            ref,
            part_s.at[a, k],
            part_r.at[a, k],
            device_id={"parts": lax.rem(me_p + k, n_parts)},
            device_id_type=MESH,
        )

    @pl.when(has_up)
    def _():
        z_copy(me_z, me_z + 1, up_s).start()

    @pl.when(has_dn)
    def _():
        z_copy(me_z, me_z - 1, dn_s).start()

    def relay(k):
        below, above = me_z - k, me_z + k

        @pl.when(below >= 0)
        def _():
            z_copy(below, me_z, up_s).wait_recv()

            @pl.when(has_up)
            def _():
                z_copy(below, me_z + 1, up_s).start()

            for q in range(1, n_parts):
                part_copy(below, q).start()

        @pl.when(above < n_dp)
        def _():
            z_copy(above, me_z, dn_s).wait_recv()

            @pl.when(has_dn)
            def _():
                z_copy(above, me_z - 1, dn_s).start()

            for q in range(1, n_parts):
                part_copy(above, q).start()

    def pair_copy(d, i):
        at = pl.ds(pl.multiple_of(i * chunk, chunk), chunk)
        return pltpu.make_async_remote_copy(
            pair_out.at[d, at],
            pair_in.at[d, at],
            pair_s.at[d, i],
            pair_r.at[d, i],
            device_id={"mp": mate},
            device_id_type=MESH,
        )

    def far_copy(d, i):
        at = pl.ds(pl.multiple_of(i * chunk, chunk), chunk)
        return pltpu.make_async_remote_copy(
            far_out.at[d - 1, at],
            far_in.at[d - 1, at],
            far_s.at[d - 1, i],
            far_r.at[d - 1, i],
            device_id={"mp": far_id(d)},
            device_id_type=MESH,
        )

    def forward(d, i):
        at = pl.ds(pl.multiple_of(i * chunk, chunk), chunk)
        pair_copy(d, i).wait_recv()
        far_out[d - 1, at] = (acc[d, at] + pair_in[d, at].astype(F32)).astype(BF16)
        far_copy(d, i).start()

    def base_step(n, d, i):
        at = pl.ds(i * chunk, chunk)
        if i == 0:
            w_copy(*w_list[2 * n]).wait()
        if n == 0:
            tok_copy(i).wait()
            scaled[at] = tok[at] * gain_ref[...].reshape(1, feats)
        pair_out[d, at] = jnp.dot(scaled[at], w[2 * n], preferred_element_type=F32).astype(BF16)
        pair_copy(d, i).start()
        if i == 0:
            w_copy(*w_list[2 * n + 1]).wait()
        acc[d, at] = jnp.dot(scaled[at], w[2 * n + 1], preferred_element_type=F32)
        if d > 0 and i > 0:
            forward(d, i - 1)

    for n, d in enumerate(order[:-1]):
        for i in range(chunks):
            base_step(n, d, i)
            if n == 0 and i == chunks // 2:
                relay(1)
        forward(d, chunks - 1)

    ones = jnp.ones((feats, TILE), BF16)
    for i in range(chunks):
        at = pl.ds(i * chunk, chunk)
        sq_cols[at] = jnp.dot(tok[at] * tok[at], ones, preferred_element_type=F32)
    for t in range(tiles):
        sq[0, t : t + 1, :] = sq_cols[t * TILE : (t + 1) * TILE, :].T[0:1, :]
    for k in range(1, n_mp):
        sq_copy(sq, sq_s, sq_r, me, n_mp, k).start()
    if n_dp > 2:
        relay(2)
    for i in range(chunks):
        base_step(xs - 1, 0, i)
        if i == chunks // 2 - 1:
            for k in range(3, n_dp):
                relay(k)

    for a in range(n_dp):

        @pl.when(me_z != a)
        def _(a=a):
            for q in range(1, n_parts):
                other = lax.rem(me_p + n_parts - q, n_parts)
                ref = part_of(a, other)
                pltpu.make_async_remote_copy(
                    ref,
                    ref,
                    part_s.at[a, q],
                    part_r.at[a, q],
                    device_id={"parts": lax.rem(me_p + q, n_parts)},
                    device_id_type=MESH,
                ).wait_recv()

    lane = lax.broadcasted_iota(jnp.int32, (TILE, lanes), 1)
    upper = lane >= rank
    slots = [store_ref[owner_ref[t]] for t in range(tiles)]

    for i in range(chunks):
        low_all = lax.dot_general(
            scaled[pl.ds(i * chunk, chunk)],
            gath[:, :feats],
            (((1,), (1,)), ((), ())),
            preferred_element_type=F32,
        )
        for t in range(i * chunk // TILE, (i + 1) * chunk // TILE):
            first = t * TILE - i * chunk
            low = low_all[first : first + TILE]
            picked = jnp.zeros((TILE, lanes), F32)
            for g in range(n_dp // 2):
                picked = jnp.where(
                    2 * g + upper.astype(jnp.int32) == slots[t],
                    low[:, g * lanes : (g + 1) * lanes],
                    picked,
                )
            low_sel[t * TILE : (t + 1) * TILE] = picked + pltpu.roll(picked, rank, 1)

    quarter = tiles // 4
    for h in range(CORES):
        for q in range(quarter):
            first = h * (tiles // 2) + q
            second = first + quarter
            low_pack[h, q * TILE : (q + 1) * TILE, :] = jnp.where(
                upper,
                low_sel[second * TILE : (second + 1) * TILE, :],
                low_sel[first * TILE : (first + 1) * TILE, :],
            ).astype(BF16)
    to_mate = pltpu.make_async_remote_copy(
        low_pack.at[1 - c],
        low_pair,
        low_s.at[0],
        low_r.at[0],
        device_id={"mp": mate},
        device_id_type=MESH,
    )
    to_mate.start()
    to_mate.wait_recv()
    low_far_out[...] = (low_pack[c].astype(F32) + low_pair[...].astype(F32)).astype(BF16)

    def low_far(d):
        return pltpu.make_async_remote_copy(
            low_far_out,
            low_far_in.at[d - 1],
            lowx_s.at[d - 1],
            lowx_r.at[d - 1],
            device_id={"mp": far_id(d)},
            device_id_type=MESH,
        )

    for d in range(1, xs):
        low_far(d).start()

    for i in range(chunks):
        at = pl.ds(i * chunk, chunk)
        pair_copy(0, i).wait_recv()
        acc[0, at] = acc[0, at] + pair_in[0, at].astype(F32)
    total = sq[0]
    for k in range(1, n_mp):
        sq_copy(sq, sq_s, sq_r, me, n_mp, k).wait_recv()
        total = total + sq[k]
    inv = lax.rsqrt(total / (feats * n_mp) + 1e-05)
    sq_cols[...] = jnp.concatenate(
        [jnp.broadcast_to(inv[t : t + 1, :], (TILE, TILE)).T for t in range(tiles)], axis=0
    )

    low_sum = low_far_out[...].astype(F32)
    for d in range(1, xs):
        low_far(d).wait_recv()
        low_sum = low_sum + low_far_in[d - 1].astype(F32)
    low_done[c] = low_sum.astype(BF16)
    done = pltpu.make_async_remote_copy(
        low_done.at[c],
        low_done.at[c],
        low_s.at[1],
        low_r.at[1],
        device_id={"mp": mate},
        device_id_type=MESH,
    )
    done.start()
    pltpu.make_async_remote_copy(
        low_done.at[1 - c],
        low_done.at[1 - c],
        low_s.at[1],
        low_r.at[1],
        device_id={"mp": mate},
        device_id_type=MESH,
    ).wait_recv()

    for t in range(tiles):
        at = slice(t * TILE, (t + 1) * TILE)
        h, j = t // (tiles // 2), t % (tiles // 2)
        q, second = j % quarter, j >= quarter
        packed = low_done[h, q * TILE : (q + 1) * TILE, :].astype(F32)
        rolled = pltpu.roll(packed, rank, 1)
        own = jnp.where(upper, packed, rolled) if second else jnp.where(upper, rolled, packed)
        spread = jnp.concatenate(
            [
                jnp.where(2 * g + upper.astype(jnp.int32) == slots[t], own, 0.0)
                for g in range(n_dp // 2)
            ],
            axis=1,
        ).astype(BF16)
        delta = jnp.dot(spread, gath[:, feats:], preferred_element_type=F32)
        acc[0, at] = acc[0, at] + 2.0 * delta

    for i in range(chunks):
        for d in range(1, xs):
            far_copy(d, i).wait_recv()
        for t in range(i * chunk // TILE, (i + 1) * chunk // TILE):
            at = slice(t * TILE, (t + 1) * TILE)
            value = acc[0, at]
            for d in range(1, xs):
                value = value + far_in[d - 1, at].astype(F32)
            scale = jnp.concatenate([sq_cols[at, :]] * (block // TILE), axis=1)
            out_ref[at, :] = jnp.where(t < count_ref[0], value * scale, 0.0).astype(BF16)

    for d in order:
        for i in range(chunks):
            pair_copy(d, i).wait_send()
            if d > 0:
                far_copy(d, i).wait_send()
    for k in range(1, n_mp):
        sq_copy(sq, sq_s, sq_r, me, n_mp, k).wait_send()
    to_mate.wait_send()
    done.wait_send()
    for d in range(1, xs):
        low_far(d).wait_send()
    for a in range(n_dp):

        @pl.when(jnp.logical_and(has_up, a <= me_z))
        def _(a=a):
            z_copy(a, me_z, up_s).wait_send()

        @pl.when(jnp.logical_and(has_dn, a >= me_z))
        def _(a=a):
            z_copy(a, me_z, dn_s).wait_send()

        @pl.when(me_z != a)
        def _(a=a):
            for q in range(1, n_parts):
                part_copy(a, q).wait_send()


def sq_copy(sq, sq_s, sq_r, me, n_mp, k):
    return pltpu.make_async_remote_copy(
        sq.at[0],
        sq.at[k],
        sq_s.at[k],
        sq_r.at[k],
        device_id={"mp": lax.rem(me + k, n_mp)},
        device_id_type=MESH,
    )


def shards(mesh, tokens, gain, weight, down, up, owner, count, store):
    n_parts, n_dp, n_mp = (mesh.shape[name] for name in ("parts", "dp", "mp"))
    rows, feats = tokens.shape
    cols = weight.shape[1]
    rank = down.shape[2]
    block = cols // n_mp
    xs = n_mp // CORES
    chunk = 256
    chunks = rows // chunk
    far = max(xs - 1, 1)
    low_rows = rows // 4
    vmem = pltpu.VMEM
    dma = pltpu.SemaphoreType.DMA
    smem = pl.BlockSpec(memory_space=pltpu.SMEM)
    in_vmem = pl.BlockSpec(memory_space=pltpu.VMEM)
    in_hbm = pl.BlockSpec(memory_space=pl.ANY)
    return pl.pallas_call(
        functools.partial(kernel, (n_parts, n_dp, n_mp, chunk)),
        out_shape=jax.ShapeDtypeStruct((rows, block), BF16),
        in_specs=[smem, smem, smem, in_hbm, in_vmem, in_hbm, in_vmem, in_vmem],
        out_specs=in_vmem,
        scratch_shapes=[
            vmem((rows, feats), BF16),
            vmem((rows, feats), BF16),
            vmem((n_mp, feats, block), BF16),
            vmem((n_dp * rank, feats + block), BF16),
            vmem((xs, rows, block), BF16),
            vmem((xs, rows, block), BF16),
            vmem((xs, rows, block), F32),
            vmem((far, rows, block), BF16),
            vmem((far, rows, block), BF16),
            vmem((rows, TILE), F32),
            vmem((n_mp, rows // TILE, TILE), F32),
            vmem((rows, 2 * rank), F32),
            vmem((CORES, low_rows, 2 * rank), BF16),
            vmem((low_rows, 2 * rank), BF16),
            vmem((low_rows, 2 * rank), BF16),
            vmem((far, low_rows, 2 * rank), BF16),
            vmem((CORES, low_rows, 2 * rank), BF16),
            dma((chunks,)),
            dma((n_mp,)),
            dma((xs, chunks)),
            dma((xs, chunks)),
            dma((far, chunks)),
            dma((far, chunks)),
            dma((n_mp,)),
            dma((n_mp,)),
            dma((n_dp,)),
            dma((n_dp,)),
            dma((n_dp,)),
            dma((n_dp, n_parts)),
            dma((n_dp, n_parts)),
            dma((2,)),
            dma((2,)),
            dma((far,)),
            dma((far,)),
        ],
        compiler_params=pltpu.CompilerParams(
            collective_id=0, has_side_effects=True, vmem_limit_bytes=56 * 1024 * 1024
        ),
    )(owner, count, store, tokens, gain, weight, down.transpose(0, 2, 1), up)


def solution(mesh):
    in_specs = (
        P(("parts", "dp"), "mp"),
        P("mp"),
        P("mp", None),
        P("dp", "mp", None),
        P("dp", None, "mp"),
        P(("parts", "dp")),
        P(("parts", "dp")),
        P(),
    )
    out_specs = P(("parts", "dp"), "mp")
    return jax.shard_map(
        functools.partial(shards, mesh),
        mesh=mesh,
        in_specs=in_specs,
        out_specs=out_specs,
        check_vma=False,
    )
```

```python
import functools

import jax
import jax.numpy as jnp
from jax import lax
from jax.experimental import pallas as pl
from jax.experimental.pallas import tpu as pltpu
from jax.sharding import PartitionSpec as P

TILE = 128
CORES = 2
SUBS = 2
MESH = pl.DeviceIdType.MESH
F32 = jnp.float32
BF16 = jnp.bfloat16


def kernel(
    sizes,
    owner_ref,
    count_ref,
    store_ref,
    tok_hbm,
    gain_ref,
    w_hbm,
    down_ref,
    up_ref,
    out_ref,
    tok,
    scaled,
    w,
    gath,
    pair_out,
    pair_in,
    acc,
    far_out,
    far_in,
    sq_cols,
    sq,
    low_sel,
    low_pack,
    low_pair,
    low_far_out,
    low_far_in,
    low_done,
    tok_sem,
    w_sem,
    pair_s,
    pair_r,
    far_s,
    far_r,
    sq_s,
    sq_r,
    up_s,
    dn_s,
    z_r,
    part_s,
    part_r,
    low_s,
    low_r,
    lowx_s,
    lowx_r,
):
    n_parts, n_dp, n_mp, chunk = sizes
    rows, feats = tok.shape
    block = w.shape[2]
    rank = down_ref.shape[1]
    lanes = 2 * rank
    xs = n_mp // CORES
    chunks = rows // chunk
    tiles = rows // TILE
    me_p, me_z, me = lax.axis_index("parts"), lax.axis_index("dp"), lax.axis_index("mp")
    x, c = me // CORES, me % CORES
    mate = x * CORES + (1 - c)

    def far_id(d):
        return lax.rem(x + d, xs) * CORES + c

    def col(d, core):
        return lax.rem(x + d, xs) * CORES + core

    def tok_copy(i):
        at = pl.ds(pl.multiple_of(i * chunk, chunk), chunk)
        return pltpu.make_async_copy(tok_hbm.at[at], tok.at[at], tok_sem.at[i])

    def w_copy(k, index):
        at = pl.ds(pl.multiple_of(index * block, block), block)
        return pltpu.make_async_copy(w_hbm.at[:, at], w.at[k], w_sem.at[k])

    order = list(range(1, xs)) + [0]
    w_list = []
    for d in order:
        for core in (1 - c, c):
            w_list.append((len(w_list), col(d, core)))
    tok_copy(0).start()
    w_copy(*w_list[0]).start()
    w_copy(*w_list[1]).start()
    for i in range(1, chunks):
        tok_copy(i).start()
    for item in w_list[2:]:
        w_copy(*item).start()

    barrier = pltpu.get_barrier_semaphore()
    has_up = me_z < n_dp - 1
    has_dn = me_z > 0
    for k in range(1, n_mp):
        pl.semaphore_signal(
            barrier, inc=1, device_id={"mp": lax.rem(me + k, n_mp)}, device_id_type=MESH
        )
    for k in range(1, n_parts):
        pl.semaphore_signal(
            barrier, inc=1, device_id={"parts": lax.rem(me_p + k, n_parts)}, device_id_type=MESH
        )

    @pl.when(has_up)
    def _():
        pl.semaphore_signal(barrier, inc=1, device_id={"dp": me_z + 1}, device_id_type=MESH)

    @pl.when(has_dn)
    def _():
        pl.semaphore_signal(barrier, inc=1, device_id={"dp": me_z - 1}, device_id_type=MESH)

    chain = has_up.astype(jnp.int32) + has_dn.astype(jnp.int32)
    pl.semaphore_wait(barrier, n_mp - 1 + n_parts - 1 + chain)

    own_rows = pl.ds(pl.multiple_of(me_z * rank, rank), rank)
    gath[own_rows, :feats] = down_ref[0]
    gath[own_rows, feats:] = up_ref[0]
    piece = rank // n_parts // SUBS

    def part_of(a, p, s):
        return gath.at[pl.ds(pl.multiple_of(a * rank + (p * SUBS + s) * piece, 16), piece)]

    def z_copy(a, to, sems, s):
        ref = part_of(a, me_p, s)
        return pltpu.make_async_remote_copy(
            ref, ref, sems.at[a, s], z_r.at[a, s], device_id={"dp": to}, device_id_type=MESH
        )

    def part_copy(a, k, s):
        ref = part_of(a, me_p, s)
        return pltpu.make_async_remote_copy(
            ref,
            ref,
            part_s.at[a, k, s],
            part_r.at[a, k, s],
            device_id={"parts": lax.rem(me_p + k, n_parts)},
            device_id_type=MESH,
        )

    @pl.when(has_up)
    def _():
        for s in range(SUBS):
            z_copy(me_z, me_z + 1, up_s, s).start()

    @pl.when(has_dn)
    def _():
        for s in range(SUBS):
            z_copy(me_z, me_z - 1, dn_s, s).start()

    def relay(k, s):
        below, above = me_z - k, me_z + k

        @pl.when(below >= 0)
        def _():
            z_copy(below, me_z, up_s, s).wait_recv()

            @pl.when(has_up)
            def _():
                z_copy(below, me_z + 1, up_s, s).start()

            for q in range(1, n_parts):
                part_copy(below, q, s).start()

        @pl.when(above < n_dp)
        def _():
            z_copy(above, me_z, dn_s, s).wait_recv()

            @pl.when(has_dn)
            def _():
                z_copy(above, me_z - 1, dn_s, s).start()

            for q in range(1, n_parts):
                part_copy(above, q, s).start()

    def pair_copy(d, i):
        at = pl.ds(pl.multiple_of(i * chunk, chunk), chunk)
        return pltpu.make_async_remote_copy(
            pair_out.at[d, at],
            pair_in.at[d, at],
            pair_s.at[d, i],
            pair_r.at[d, i],
            device_id={"mp": mate},
            device_id_type=MESH,
        )

    def far_copy(d, i):
        at = pl.ds(pl.multiple_of(i * chunk, chunk), chunk)
        return pltpu.make_async_remote_copy(
            far_out.at[d - 1, at],
            far_in.at[d - 1, at],
            far_s.at[d - 1, i],
            far_r.at[d - 1, i],
            device_id={"mp": far_id(d)},
            device_id_type=MESH,
        )

    def forward(d, i):
        at = pl.ds(pl.multiple_of(i * chunk, chunk), chunk)
        pair_copy(d, i).wait_recv()
        far_out[d - 1, at] = (acc[d, at] + pair_in[d, at].astype(F32)).astype(BF16)
        far_copy(d, i).start()

    def base_step(n, d, i):
        at = pl.ds(i * chunk, chunk)
        if i == 0:
            w_copy(*w_list[2 * n]).wait()
        if n == 0:
            tok_copy(i).wait()
            scaled[at] = tok[at] * gain_ref[...].reshape(1, feats)
        pair_out[d, at] = jnp.dot(scaled[at], w[2 * n], preferred_element_type=F32).astype(BF16)
        pair_copy(d, i).start()
        if i == 0:
            w_copy(*w_list[2 * n + 1]).wait()
        acc[d, at] = jnp.dot(scaled[at], w[2 * n + 1], preferred_element_type=F32)
        if d > 0 and i > 0:
            forward(d, i - 1)

    for n, d in enumerate(order[:-1]):
        for i in range(chunks):
            base_step(n, d, i)
            if n == 0 and i == chunks // 2 - 1:
                relay(1, 0)
            if n == 0 and i == chunks // 2:
                relay(1, 1)
        forward(d, chunks - 1)

    if n_dp > 2:
        relay(2, 0)

    ones = jnp.ones((feats, TILE), BF16)
    for i in range(chunks):
        at = pl.ds(i * chunk, chunk)
        sq_cols[at] = jnp.dot(tok[at] * tok[at], ones, preferred_element_type=F32)
    for t in range(tiles):
        sq[0, t : t + 1, :] = sq_cols[t * TILE : (t + 1) * TILE, :].T[0:1, :]
    for k in range(1, n_mp):
        sq_copy(sq, sq_s, sq_r, me, n_mp, k).start()
    if n_dp > 2:
        relay(2, 1)
    for i in range(chunks):
        base_step(xs - 1, 0, i)
        if n_dp > 3 and i == chunks // 2 - 2:
            relay(3, 0)
        if n_dp > 3 and i == chunks // 2 - 1:
            relay(3, 1)
            for k in range(4, n_dp):
                for s in range(SUBS):
                    relay(k, s)

    for a in range(n_dp):

        @pl.when(me_z != a)
        def _(a=a):
            for q in range(1, n_parts):
                other = lax.rem(me_p + n_parts - q, n_parts)
                for s in range(SUBS):
                    ref = part_of(a, other, s)
                    pltpu.make_async_remote_copy(
                        ref,
                        ref,
                        part_s.at[a, q, s],
                        part_r.at[a, q, s],
                        device_id={"parts": lax.rem(me_p + q, n_parts)},
                        device_id_type=MESH,
                    ).wait_recv()

    lane = lax.broadcasted_iota(jnp.int32, (TILE, lanes), 1)
    upper = lane >= rank
    slots = [store_ref[owner_ref[t]] for t in range(tiles)]

    for i in range(chunks):
        low_all = lax.dot_general(
            scaled[pl.ds(i * chunk, chunk)],
            gath[:, :feats],
            (((1,), (1,)), ((), ())),
            preferred_element_type=F32,
        )
        for t in range(i * chunk // TILE, (i + 1) * chunk // TILE):
            first = t * TILE - i * chunk
            low = low_all[first : first + TILE]
            picked = jnp.zeros((TILE, lanes), F32)
            for g in range(n_dp // 2):
                picked = jnp.where(
                    2 * g + upper.astype(jnp.int32) == slots[t],
                    low[:, g * lanes : (g + 1) * lanes],
                    picked,
                )
            low_sel[t * TILE : (t + 1) * TILE] = picked + pltpu.roll(picked, rank, 1)

    quarter = tiles // 4
    for h in range(CORES):
        for q in range(quarter):
            first = h * (tiles // 2) + q
            second = first + quarter
            low_pack[h, q * TILE : (q + 1) * TILE, :] = jnp.where(
                upper,
                low_sel[second * TILE : (second + 1) * TILE, :],
                low_sel[first * TILE : (first + 1) * TILE, :],
            ).astype(BF16)
    to_mate = pltpu.make_async_remote_copy(
        low_pack.at[1 - c],
        low_pair,
        low_s.at[0],
        low_r.at[0],
        device_id={"mp": mate},
        device_id_type=MESH,
    )
    to_mate.start()
    to_mate.wait_recv()
    low_far_out[...] = (low_pack[c].astype(F32) + low_pair[...].astype(F32)).astype(BF16)

    def low_far(d):
        return pltpu.make_async_remote_copy(
            low_far_out,
            low_far_in.at[d - 1],
            lowx_s.at[d - 1],
            lowx_r.at[d - 1],
            device_id={"mp": far_id(d)},
            device_id_type=MESH,
        )

    for d in range(1, xs):
        low_far(d).start()

    for i in range(chunks):
        at = pl.ds(i * chunk, chunk)
        pair_copy(0, i).wait_recv()
        acc[0, at] = acc[0, at] + pair_in[0, at].astype(F32)
    total = sq[0]
    for k in range(1, n_mp):
        sq_copy(sq, sq_s, sq_r, me, n_mp, k).wait_recv()
        total = total + sq[k]
    inv = lax.rsqrt(total / (feats * n_mp) + 1e-05)
    sq_cols[...] = jnp.concatenate(
        [jnp.broadcast_to(inv[t : t + 1, :], (TILE, TILE)).T for t in range(tiles)], axis=0
    )

    low_sum = low_far_out[...].astype(F32)
    for d in range(1, xs):
        low_far(d).wait_recv()
        low_sum = low_sum + low_far_in[d - 1].astype(F32)
    low_done[c] = low_sum.astype(BF16)
    done = pltpu.make_async_remote_copy(
        low_done.at[c],
        low_done.at[c],
        low_s.at[1],
        low_r.at[1],
        device_id={"mp": mate},
        device_id_type=MESH,
    )
    done.start()
    pltpu.make_async_remote_copy(
        low_done.at[1 - c],
        low_done.at[1 - c],
        low_s.at[1],
        low_r.at[1],
        device_id={"mp": mate},
        device_id_type=MESH,
    ).wait_recv()

    for t in range(tiles):
        at = slice(t * TILE, (t + 1) * TILE)
        h, j = t // (tiles // 2), t % (tiles // 2)
        q, second = j % quarter, j >= quarter
        packed = low_done[h, q * TILE : (q + 1) * TILE, :].astype(F32)
        rolled = pltpu.roll(packed, rank, 1)
        own = jnp.where(upper, packed, rolled) if second else jnp.where(upper, rolled, packed)
        spread = jnp.concatenate(
            [
                jnp.where(2 * g + upper.astype(jnp.int32) == slots[t], own, 0.0)
                for g in range(n_dp // 2)
            ],
            axis=1,
        ).astype(BF16)
        delta = jnp.dot(spread, gath[:, feats:], preferred_element_type=F32)
        acc[0, at] = acc[0, at] + 2.0 * delta

    for i in range(chunks):
        for d in range(1, xs):
            far_copy(d, i).wait_recv()
        for t in range(i * chunk // TILE, (i + 1) * chunk // TILE):
            at = slice(t * TILE, (t + 1) * TILE)
            value = acc[0, at]
            for d in range(1, xs):
                value = value + far_in[d - 1, at].astype(F32)
            scale = jnp.concatenate([sq_cols[at, :]] * (block // TILE), axis=1)
            out_ref[at, :] = jnp.where(t < count_ref[0], value * scale, 0.0).astype(BF16)

    for d in order:
        for i in range(chunks):
            pair_copy(d, i).wait_send()
            if d > 0:
                far_copy(d, i).wait_send()
    for k in range(1, n_mp):
        sq_copy(sq, sq_s, sq_r, me, n_mp, k).wait_send()
    to_mate.wait_send()
    done.wait_send()
    for d in range(1, xs):
        low_far(d).wait_send()
    for a in range(n_dp):

        @pl.when(jnp.logical_and(has_up, a <= me_z))
        def _(a=a):
            for s in range(SUBS):
                z_copy(a, me_z, up_s, s).wait_send()

        @pl.when(jnp.logical_and(has_dn, a >= me_z))
        def _(a=a):
            for s in range(SUBS):
                z_copy(a, me_z, dn_s, s).wait_send()

        @pl.when(me_z != a)
        def _(a=a):
            for q in range(1, n_parts):
                for s in range(SUBS):
                    part_copy(a, q, s).wait_send()


def sq_copy(sq, sq_s, sq_r, me, n_mp, k):
    return pltpu.make_async_remote_copy(
        sq.at[0],
        sq.at[k],
        sq_s.at[k],
        sq_r.at[k],
        device_id={"mp": lax.rem(me + k, n_mp)},
        device_id_type=MESH,
    )


def shards(mesh, tokens, gain, weight, down, up, owner, count, store):
    n_parts, n_dp, n_mp = (mesh.shape[name] for name in ("parts", "dp", "mp"))
    rows, feats = tokens.shape
    cols = weight.shape[1]
    rank = down.shape[2]
    block = cols // n_mp
    xs = n_mp // CORES
    chunk = 256
    chunks = rows // chunk
    far = max(xs - 1, 1)
    low_rows = rows // 4
    vmem = pltpu.VMEM
    dma = pltpu.SemaphoreType.DMA
    smem = pl.BlockSpec(memory_space=pltpu.SMEM)
    in_vmem = pl.BlockSpec(memory_space=pltpu.VMEM)
    in_hbm = pl.BlockSpec(memory_space=pl.ANY)
    return pl.pallas_call(
        functools.partial(kernel, (n_parts, n_dp, n_mp, chunk)),
        out_shape=jax.ShapeDtypeStruct((rows, block), BF16),
        in_specs=[smem, smem, smem, in_hbm, in_vmem, in_hbm, in_vmem, in_vmem],
        out_specs=in_vmem,
        scratch_shapes=[
            vmem((rows, feats), BF16),
            vmem((rows, feats), BF16),
            vmem((n_mp, feats, block), BF16),
            vmem((n_dp * rank, feats + block), BF16),
            vmem((xs, rows, block), BF16),
            vmem((xs, rows, block), BF16),
            vmem((xs, rows, block), F32),
            vmem((far, rows, block), BF16),
            vmem((far, rows, block), BF16),
            vmem((rows, TILE), F32),
            vmem((n_mp, rows // TILE, TILE), F32),
            vmem((rows, 2 * rank), F32),
            vmem((CORES, low_rows, 2 * rank), BF16),
            vmem((low_rows, 2 * rank), BF16),
            vmem((low_rows, 2 * rank), BF16),
            vmem((far, low_rows, 2 * rank), BF16),
            vmem((CORES, low_rows, 2 * rank), BF16),
            dma((chunks,)),
            dma((n_mp,)),
            dma((xs, chunks)),
            dma((xs, chunks)),
            dma((far, chunks)),
            dma((far, chunks)),
            dma((n_mp,)),
            dma((n_mp,)),
            dma((n_dp, SUBS)),
            dma((n_dp, SUBS)),
            dma((n_dp, SUBS)),
            dma((n_dp, n_parts, SUBS)),
            dma((n_dp, n_parts, SUBS)),
            dma((2,)),
            dma((2,)),
            dma((far,)),
            dma((far,)),
        ],
        compiler_params=pltpu.CompilerParams(
            collective_id=0, has_side_effects=True, vmem_limit_bytes=56 * 1024 * 1024
        ),
    )(owner, count, store, tokens, gain, weight, down.transpose(0, 2, 1), up)


def solution(mesh):
    in_specs = (
        P(("parts", "dp"), "mp"),
        P("mp"),
        P("mp", None),
        P("dp", "mp", None),
        P("dp", None, "mp"),
        P(("parts", "dp")),
        P(("parts", "dp")),
        P(),
    )
    out_specs = P(("parts", "dp"), "mp")
    return jax.shard_map(
        functools.partial(shards, mesh),
        mesh=mesh,
        in_specs=in_specs,
        out_specs=out_specs,
        check_vma=False,
    )
```

```python
import functools

import jax
import jax.numpy as jnp
from jax import lax
from jax.experimental import pallas as pl
from jax.experimental.pallas import tpu as pltpu
from jax.sharding import PartitionSpec as P

TILE = 128
CORES = 2
SUBS = 2
MESH = pl.DeviceIdType.MESH
F32 = jnp.float32
BF16 = jnp.bfloat16


def kernel(
    sizes,
    owner_ref,
    count_ref,
    store_ref,
    tok_hbm,
    gain_ref,
    w_hbm,
    down_ref,
    up_ref,
    out_ref,
    tok,
    scaled,
    w,
    gath,
    pair_out,
    pair_in,
    acc,
    far_out,
    far_in,
    sq_cols,
    sq,
    low_sel,
    low_pack,
    low_pair,
    low_far_out,
    low_far_in,
    low_done,
    tok_sem,
    w_sem,
    pair_s,
    pair_r,
    far_s,
    far_r,
    sq_s,
    sq_r,
    up_s,
    dn_s,
    z_r,
    part_s,
    part_r,
    low_s,
    low_r,
    lowx_s,
    lowx_r,
):
    n_parts, n_dp, n_mp, chunk = sizes
    rows, feats = tok.shape
    block = w.shape[2]
    rank = down_ref.shape[1]
    lanes = 2 * rank
    xs = n_mp // CORES
    chunks = rows // chunk
    tiles = rows // TILE
    me_p, me_z, me = lax.axis_index("parts"), lax.axis_index("dp"), lax.axis_index("mp")
    x, c = me // CORES, me % CORES
    mate = x * CORES + (1 - c)

    def far_id(d):
        return lax.rem(x + d, xs) * CORES + c

    def col(d, core):
        return lax.rem(x + d, xs) * CORES + core

    def tok_copy(i):
        at = pl.ds(pl.multiple_of(i * chunk, chunk), chunk)
        return pltpu.make_async_copy(tok_hbm.at[at], tok.at[at], tok_sem.at[i])

    def w_copy(k, index):
        at = pl.ds(pl.multiple_of(index * block, block), block)
        return pltpu.make_async_copy(w_hbm.at[:, at], w.at[k], w_sem.at[k])

    order = list(range(1, xs)) + [0]
    w_list = []
    for d in order:
        for core in (1 - c, c):
            w_list.append((len(w_list), col(d, core)))
    tok_copy(0).start()
    w_copy(*w_list[0]).start()
    w_copy(*w_list[1]).start()
    for i in range(1, chunks):
        tok_copy(i).start()
    for item in w_list[2:]:
        w_copy(*item).start()

    barrier = pltpu.get_barrier_semaphore()
    has_up = me_z < n_dp - 1
    has_dn = me_z > 0
    for k in range(1, n_mp):
        pl.semaphore_signal(
            barrier, inc=1, device_id={"mp": lax.rem(me + k, n_mp)}, device_id_type=MESH
        )
    for k in range(1, n_parts):
        pl.semaphore_signal(
            barrier, inc=1, device_id={"parts": lax.rem(me_p + k, n_parts)}, device_id_type=MESH
        )

    @pl.when(has_up)
    def _():
        pl.semaphore_signal(barrier, inc=1, device_id={"dp": me_z + 1}, device_id_type=MESH)

    @pl.when(has_dn)
    def _():
        pl.semaphore_signal(barrier, inc=1, device_id={"dp": me_z - 1}, device_id_type=MESH)

    chain = has_up.astype(jnp.int32) + has_dn.astype(jnp.int32)
    pl.semaphore_wait(barrier, n_mp - 1 + n_parts - 1 + chain)

    own_rows = pl.ds(pl.multiple_of(me_z * rank, rank), rank)
    gath[own_rows, :feats] = down_ref[0]
    gath[own_rows, feats:] = up_ref[0]
    piece = rank // n_parts // SUBS

    def part_of(a, p, s):
        return gath.at[pl.ds(pl.multiple_of(a * rank + (p * SUBS + s) * piece, 16), piece)]

    def z_copy(a, to, sems, s):
        ref = part_of(a, me_p, s)
        return pltpu.make_async_remote_copy(
            ref, ref, sems.at[a, s], z_r.at[a, s], device_id={"dp": to}, device_id_type=MESH
        )

    def part_copy(a, k, s):
        ref = part_of(a, me_p, s)
        return pltpu.make_async_remote_copy(
            ref,
            ref,
            part_s.at[a, k, s],
            part_r.at[a, k, s],
            device_id={"parts": lax.rem(me_p + k, n_parts)},
            device_id_type=MESH,
        )

    @pl.when(has_up)
    def _():
        for s in range(SUBS):
            z_copy(me_z, me_z + 1, up_s, s).start()

    @pl.when(has_dn)
    def _():
        for s in range(SUBS):
            z_copy(me_z, me_z - 1, dn_s, s).start()

    def relay(k, s):
        below, above = me_z - k, me_z + k

        @pl.when(below >= 0)
        def _():
            z_copy(below, me_z, up_s, s).wait_recv()

            @pl.when(has_up)
            def _():
                z_copy(below, me_z + 1, up_s, s).start()

            for q in range(1, n_parts):
                part_copy(below, q, s).start()

        @pl.when(above < n_dp)
        def _():
            z_copy(above, me_z, dn_s, s).wait_recv()

            @pl.when(has_dn)
            def _():
                z_copy(above, me_z - 1, dn_s, s).start()

            for q in range(1, n_parts):
                part_copy(above, q, s).start()

    def pair_copy(d, i):
        at = pl.ds(pl.multiple_of(i * chunk, chunk), chunk)
        return pltpu.make_async_remote_copy(
            pair_out.at[d, at],
            pair_in.at[d, at],
            pair_s.at[d, i],
            pair_r.at[d, i],
            device_id={"mp": mate},
            device_id_type=MESH,
        )

    def far_copy(d, i):
        at = pl.ds(pl.multiple_of(i * chunk, chunk), chunk)
        return pltpu.make_async_remote_copy(
            far_out.at[d - 1, at],
            far_in.at[d - 1, at],
            far_s.at[d - 1, i],
            far_r.at[d - 1, i],
            device_id={"mp": far_id(d)},
            device_id_type=MESH,
        )

    def forward(d, i):
        at = pl.ds(pl.multiple_of(i * chunk, chunk), chunk)
        pair_copy(d, i).wait_recv()
        far_out[d - 1, at] = (acc[d, at] + pair_in[d, at].astype(F32)).astype(BF16)
        far_copy(d, i).start()

    def base_step(n, d, i):
        at = pl.ds(i * chunk, chunk)
        if i == 0:
            w_copy(*w_list[2 * n]).wait()
        if n == 0:
            tok_copy(i).wait()
            scaled[at] = tok[at] * gain_ref[...].reshape(1, feats)
        pair_out[d, at] = jnp.dot(scaled[at], w[2 * n], preferred_element_type=F32).astype(BF16)
        pair_copy(d, i).start()
        if i == 0:
            w_copy(*w_list[2 * n + 1]).wait()
        acc[d, at] = jnp.dot(scaled[at], w[2 * n + 1], preferred_element_type=F32)
        if d > 0 and i > 0:
            forward(d, i - 1)

    for n, d in enumerate(order[:-1]):
        for i in range(chunks):
            base_step(n, d, i)
            if n == 0 and i == chunks // 2 - 1:
                relay(1, 0)
            if n == 0 and i == chunks // 2:
                relay(1, 1)
        forward(d, chunks - 1)

    if n_dp > 2:
        relay(2, 0)

    ones = jnp.ones((feats, TILE), BF16)
    for i in range(chunks):
        at = pl.ds(i * chunk, chunk)
        sq_cols[at] = jnp.dot(tok[at] * tok[at], ones, preferred_element_type=F32)
    for t in range(tiles):
        sq[0, t : t + 1, :] = sq_cols[t * TILE : (t + 1) * TILE, :].T[0:1, :]
    for k in range(1, n_mp):
        sq_copy(sq, sq_s, sq_r, me, n_mp, k).start()
    if n_dp > 2:
        relay(2, 1)
    for i in range(chunks):
        base_step(xs - 1, 0, i)
        if n_dp > 3 and i == chunks // 2 - 2:
            relay(3, 0)
        if n_dp > 3 and i == chunks // 2 - 1:
            relay(3, 1)
            for k in range(4, n_dp):
                for s in range(SUBS):
                    relay(k, s)

    for a in range(n_dp):

        @pl.when(me_z != a)
        def _(a=a):
            for q in range(1, n_parts):
                other = lax.rem(me_p + n_parts - q, n_parts)
                for s in range(SUBS):
                    ref = part_of(a, other, s)
                    pltpu.make_async_remote_copy(
                        ref,
                        ref,
                        part_s.at[a, q, s],
                        part_r.at[a, q, s],
                        device_id={"parts": lax.rem(me_p + q, n_parts)},
                        device_id_type=MESH,
                    ).wait_recv()

    lane = lax.broadcasted_iota(jnp.int32, (TILE, lanes), 1)
    upper = lane >= rank
    slots = [store_ref[owner_ref[t]] for t in range(tiles)]

    for i in range(chunks):
        low_all = lax.dot_general(
            scaled[pl.ds(i * chunk, chunk)],
            gath[:, :feats],
            (((1,), (1,)), ((), ())),
            preferred_element_type=F32,
        )
        for t in range(i * chunk // TILE, (i + 1) * chunk // TILE):
            first = t * TILE - i * chunk
            low = low_all[first : first + TILE]
            picked = jnp.zeros((TILE, lanes), F32)
            for g in range(n_dp // 2):
                picked = jnp.where(
                    2 * g + upper.astype(jnp.int32) == slots[t],
                    low[:, g * lanes : (g + 1) * lanes],
                    picked,
                )
            low_sel[t * TILE : (t + 1) * TILE] = picked + pltpu.roll(picked, rank, 1)

    quarter = tiles // 4
    for h in range(CORES):
        for q in range(quarter):
            first = h * (tiles // 2) + q
            second = first + quarter
            low_pack[h, q * TILE : (q + 1) * TILE, :] = jnp.where(
                upper,
                low_sel[second * TILE : (second + 1) * TILE, :],
                low_sel[first * TILE : (first + 1) * TILE, :],
            ).astype(BF16)
    to_mate = pltpu.make_async_remote_copy(
        low_pack.at[1 - c],
        low_pair,
        low_s.at[0],
        low_r.at[0],
        device_id={"mp": mate},
        device_id_type=MESH,
    )
    to_mate.start()
    to_mate.wait_recv()
    low_far_out[...] = (low_pack[c].astype(F32) + low_pair[...].astype(F32)).astype(BF16)

    def low_far(d):
        return pltpu.make_async_remote_copy(
            low_far_out,
            low_far_in.at[d - 1],
            lowx_s.at[d - 1],
            lowx_r.at[d - 1],
            device_id={"mp": far_id(d)},
            device_id_type=MESH,
        )

    for d in range(1, xs):
        low_far(d).start()

    for i in range(chunks):
        at = pl.ds(i * chunk, chunk)
        pair_copy(0, i).wait_recv()
        value = acc[0, at] + pair_in[0, at].astype(F32)
        for d in range(1, xs):
            far_copy(d, i).wait_recv()
            value = value + far_in[d - 1, at].astype(F32)
        acc[0, at] = value
    total = sq[0]
    for k in range(1, n_mp):
        sq_copy(sq, sq_s, sq_r, me, n_mp, k).wait_recv()
        total = total + sq[k]
    inv = lax.rsqrt(total / (feats * n_mp) + 1e-05)
    sq_cols[...] = jnp.concatenate(
        [jnp.broadcast_to(inv[t : t + 1, :], (TILE, TILE)).T for t in range(tiles)], axis=0
    )

    low_sum = low_far_out[...].astype(F32)
    for d in range(1, xs):
        low_far(d).wait_recv()
        low_sum = low_sum + low_far_in[d - 1].astype(F32)
    low_done[c] = low_sum.astype(BF16)
    done = pltpu.make_async_remote_copy(
        low_done.at[c],
        low_done.at[c],
        low_s.at[1],
        low_r.at[1],
        device_id={"mp": mate},
        device_id_type=MESH,
    )
    done.start()
    pltpu.make_async_remote_copy(
        low_done.at[1 - c],
        low_done.at[1 - c],
        low_s.at[1],
        low_r.at[1],
        device_id={"mp": mate},
        device_id_type=MESH,
    ).wait_recv()

    for t in range(tiles):
        at = slice(t * TILE, (t + 1) * TILE)
        h, j = t // (tiles // 2), t % (tiles // 2)
        q, second = j % quarter, j >= quarter
        packed = low_done[h, q * TILE : (q + 1) * TILE, :].astype(F32)
        rolled = pltpu.roll(packed, rank, 1)
        own = jnp.where(upper, packed, rolled) if second else jnp.where(upper, rolled, packed)
        spread = jnp.concatenate(
            [
                jnp.where(2 * g + upper.astype(jnp.int32) == slots[t], own, 0.0)
                for g in range(n_dp // 2)
            ],
            axis=1,
        ).astype(BF16)
        delta = jnp.dot(spread, gath[:, feats:], preferred_element_type=F32)
        scale = jnp.concatenate([sq_cols[at, :]] * (block // TILE), axis=1)
        value = (acc[0, at] + 2.0 * delta) * scale
        out_ref[at, :] = jnp.where(t < count_ref[0], value, 0.0).astype(BF16)

    for d in order:
        for i in range(chunks):
            pair_copy(d, i).wait_send()
            if d > 0:
                far_copy(d, i).wait_send()
    for k in range(1, n_mp):
        sq_copy(sq, sq_s, sq_r, me, n_mp, k).wait_send()
    to_mate.wait_send()
    done.wait_send()
    for d in range(1, xs):
        low_far(d).wait_send()
    for a in range(n_dp):

        @pl.when(jnp.logical_and(has_up, a <= me_z))
        def _(a=a):
            for s in range(SUBS):
                z_copy(a, me_z, up_s, s).wait_send()

        @pl.when(jnp.logical_and(has_dn, a >= me_z))
        def _(a=a):
            for s in range(SUBS):
                z_copy(a, me_z, dn_s, s).wait_send()

        @pl.when(me_z != a)
        def _(a=a):
            for q in range(1, n_parts):
                for s in range(SUBS):
                    part_copy(a, q, s).wait_send()


def sq_copy(sq, sq_s, sq_r, me, n_mp, k):
    return pltpu.make_async_remote_copy(
        sq.at[0],
        sq.at[k],
        sq_s.at[k],
        sq_r.at[k],
        device_id={"mp": lax.rem(me + k, n_mp)},
        device_id_type=MESH,
    )


def shards(mesh, tokens, gain, weight, down, up, owner, count, store):
    n_parts, n_dp, n_mp = (mesh.shape[name] for name in ("parts", "dp", "mp"))
    rows, feats = tokens.shape
    cols = weight.shape[1]
    rank = down.shape[2]
    block = cols // n_mp
    xs = n_mp // CORES
    chunk = 256
    chunks = rows // chunk
    far = max(xs - 1, 1)
    low_rows = rows // 4
    vmem = pltpu.VMEM
    dma = pltpu.SemaphoreType.DMA
    smem = pl.BlockSpec(memory_space=pltpu.SMEM)
    in_vmem = pl.BlockSpec(memory_space=pltpu.VMEM)
    in_hbm = pl.BlockSpec(memory_space=pl.ANY)
    return pl.pallas_call(
        functools.partial(kernel, (n_parts, n_dp, n_mp, chunk)),
        out_shape=jax.ShapeDtypeStruct((rows, block), BF16),
        in_specs=[smem, smem, smem, in_hbm, in_vmem, in_hbm, in_vmem, in_vmem],
        out_specs=in_vmem,
        scratch_shapes=[
            vmem((rows, feats), BF16),
            vmem((rows, feats), BF16),
            vmem((n_mp, feats, block), BF16),
            vmem((n_dp * rank, feats + block), BF16),
            vmem((xs, rows, block), BF16),
            vmem((xs, rows, block), BF16),
            vmem((xs, rows, block), F32),
            vmem((far, rows, block), BF16),
            vmem((far, rows, block), BF16),
            vmem((rows, TILE), F32),
            vmem((n_mp, rows // TILE, TILE), F32),
            vmem((rows, 2 * rank), F32),
            vmem((CORES, low_rows, 2 * rank), BF16),
            vmem((low_rows, 2 * rank), BF16),
            vmem((low_rows, 2 * rank), BF16),
            vmem((far, low_rows, 2 * rank), BF16),
            vmem((CORES, low_rows, 2 * rank), BF16),
            dma((chunks,)),
            dma((n_mp,)),
            dma((xs, chunks)),
            dma((xs, chunks)),
            dma((far, chunks)),
            dma((far, chunks)),
            dma((n_mp,)),
            dma((n_mp,)),
            dma((n_dp, SUBS)),
            dma((n_dp, SUBS)),
            dma((n_dp, SUBS)),
            dma((n_dp, n_parts, SUBS)),
            dma((n_dp, n_parts, SUBS)),
            dma((2,)),
            dma((2,)),
            dma((far,)),
            dma((far,)),
        ],
        compiler_params=pltpu.CompilerParams(
            collective_id=0, has_side_effects=True, vmem_limit_bytes=56 * 1024 * 1024
        ),
    )(owner, count, store, tokens, gain, weight, down.transpose(0, 2, 1), up)


def solution(mesh):
    in_specs = (
        P(("parts", "dp"), "mp"),
        P("mp"),
        P("mp", None),
        P("dp", "mp", None),
        P("dp", None, "mp"),
        P(("parts", "dp")),
        P(("parts", "dp")),
        P(),
    )
    out_specs = P(("parts", "dp"), "mp")
    return jax.shard_map(
        functools.partial(shards, mesh),
        mesh=mesh,
        in_specs=in_specs,
        out_specs=out_specs,
        check_vma=False,
    )
```
